512 devices in a mesh: fsdp: 32 (over z, x_hi), tensor: 16 (over x_lo, y, core).
Axes of the slice: x: 4 (x_hi: 2, x_lo: 2; x = x_hi * 2 + x_lo), y: 4, z: 16, core: 2. Of those that a mesh axis runs over, the one named last changes fastest.
Arguments:
- grad_out: bfloat16 [512, 16384], P('fsdp', 'tensor'), may hold values from -1.1953125 to 1.1953125
- gate_pre: bfloat16 [512, 26624], P('fsdp', 'tensor'), may hold values from -6 to 6
- up_pre: bfloat16 [512, 26624], P('fsdp', 'tensor'), may hold values from -6 to 6
- down_weight: bfloat16 [26624, 16384], P('tensor', 'fsdp'), may hold values from -0.0390625 to 0.0390625
Outputs:
- grad_gate: bfloat16 [512, 26624], P('fsdp', 'tensor')
- grad_up: bfloat16 [512, 26624], P('fsdp', 'tensor')
- grad_weight: bfloat16 [26624, 16384], P('tensor', 'fsdp')
The draws below stay inside these ranges and needn't reach their ends.
All inputs are finite; a program needn't handle non-finite values.
Results may differ from the reference program's by a relative error of at most 0.0049.
Values may be sent and summed in bfloat16 or wider, within the bound.
A program may use at most 64 MiB of HBM per device.

```python
import jax
import jax.numpy as jnp
from jax import lax

D = 16384
F = 26624
TOKENS = 512
N_FSDP = 32


def block_scale(key, dims, cuts, low, top_value):
    level, own = 1.0, jax.random.fold_in(key, 6)
    for dim, blocks in cuts:
        heights = jnp.exp(jax.random.uniform(jax.random.fold_in(own, dim), (blocks,), jnp.float32, low / len(cuts), top_value / len(cuts)))
        level = level * jnp.repeat(heights, dims[dim] // blocks).reshape([-1 if axis == dim else 1 for axis in range(len(dims))])
    return level


def gaussian(stream_key, extent, spread, reach, shards=(), held_as=jnp.bfloat16):
    array = jax.random.normal(stream_key, extent, jnp.float32) * spread
    if len(shards) > 0:
        array = block_scale(stream_key, extent, shards, -0.22, 0.18) * array
    return jnp.clip(array, min=-reach, max=reach).astype(held_as)


def setup_inputs(seed: int = 0) -> dict:
    key_of = jax.random.split(jax.random.key(seed), 5)
    return {
        "grad_out": gaussian(key_of[0], (TOKENS, D), 0.2, 1.1953125, ((0, 32), (1, 16))),
        "gate_pre": gaussian(key_of[1], (TOKENS, F), 1.0, 6.0, ((0, 32), (1, 16))),
        "up_pre": gaussian(key_of[2], (TOKENS, F), 1.0, 6.0, ((0, 32), (1, 16))),
        "down_weight": gaussian(key_of[3], (F, D), F ** -0.5, 0.0390625, ((0, 16), (1, 32))),
    }


def reference(grad_out, gate_pre, up_pre, down_weight):
    gate = gate_pre.astype(jnp.float32)
    up = up_pre.astype(jnp.float32)
    hidden = (jax.nn.silu(gate) * up).astype(jnp.bfloat16)
    block = D // N_FSDP

    def add_block(total, index):
        start = (index * block).astype(jnp.int32)
        rows = lax.dynamic_slice_in_dim(grad_out, start, block, 1)
        cols = lax.dynamic_slice_in_dim(down_weight, start, block, 1)
        part = lax.dot_general(rows, cols, (((1,), (1,)), ((), ())), preferred_element_type=jnp.float32)
        return total + part, None

    grad_hidden, unused = lax.scan(add_block, jnp.zeros((TOKENS, F), jnp.float32), jnp.arange(N_FSDP, dtype=jnp.int32))
    sig = jax.nn.sigmoid(gate)
    grad_gate = (grad_hidden * up * sig * (1.0 + gate * (1.0 - sig))).astype(jnp.bfloat16)
    grad_up = (grad_hidden * gate * sig).astype(jnp.bfloat16)
    grad_weight = lax.dot_general(hidden, grad_out, (((0,), (0,)), ((), ())), preferred_element_type=jnp.float32).astype(jnp.bfloat16)
    return grad_gate, grad_up, grad_weight
```

```python
import functools

import jax
import jax.numpy as jnp
from jax import lax
from jax.experimental import pallas as pl
from jax.experimental.pallas import tpu as pltpu
from jax.sharding import PartitionSpec as P

MESH = pl.DeviceIdType.MESH
F32, BF16 = jnp.float32, jnp.bfloat16
NZ, NX, NY = 16, 2, 4
FWD, BWD = 8, 7
COLS = ((0, 896), (896, 768))


def wrap(z):
    return lax.rem(z + 2 * NZ, NZ)


def kernel(
    g_ref, gate_ref, up_ref, w_hbm, gg_ref, gu_ref, gw_hbm,
    w_ref, hid, spread, part0, part1, fa, fb, gw_ref,
    rf0, rf1, rb0, rb1, sf0, sf1, sb0, sb1, xs0, xs1, xr0, xr1,
    ag_s, ag_r, rs_s, rs_r, hx_s, hx_r, px_s, px_r, pl_s, pl_r, co_s, co_r, fx_s, fx_r, loc,
):
    f, t = lax.axis_index("fsdp"), lax.axis_index("tensor")
    z, xh = f // 2, lax.rem(f, 2)
    xl, y, core = t // (2 * NY), lax.rem(t // 2, NY), lax.rem(t, 2)
    part, rf, rb, sf, sb = (part0, part1), (rf0, rf1), (rb0, rb1), (sf0, sf1), (sb0, sb1)
    xsend, xrecv = (xs0, xs1), (xr0, xr1)

    up_z = (2 * wrap(z + 1) + xh, t)
    down_z = (2 * wrap(z - 1) + xh, t)
    x_peer = (2 * z + 1 - xh, t)
    core_peer = (f, t + 1 - 2 * core)
    plane = [(dx, dy) for dx in range(NX) for dy in range(NY) if (dx, dy) != (0, 0)]

    def chip(dx, dy):
        return lax.rem(xl + dx, NX) * 2 * NY + lax.rem(y + dy, NY) * 2

    def rows16(i):
        return pl.ds(pl.multiple_of(16 * i, 16), 16)

    def rows32(i):
        return pl.ds(pl.multiple_of(32 * i, 32), 32)

    def remote(src, dst, ss, rs, dev):
        return pltpu.make_async_remote_copy(
            src_ref=src, dst_ref=dst, send_sem=ss, recv_sem=rs, device_id=dev, device_id_type=MESH
        )

    own_diag = t == z

    bar = pltpu.get_barrier_semaphore()
    for dev in [up_z, down_z, x_peer, core_peer] + [(f, chip(dx, dy) + core) for dx, dy in plane]:
        pl.semaphore_signal(bar, inc=1, device_id=dev, device_id_type=MESH)
    for h in range(2):
        @pl.when(jnp.logical_not(own_diag & (xh == h)))
        def _():
            pl.semaphore_signal(bar, inc=1, device_id=(2 * t + h, z), device_id_type=MESH)

    w_copy = pltpu.make_async_copy(w_hbm, w_ref, loc.at[0])
    w_copy.start()

    gate, up = gate_ref[...].astype(F32), up_ref[...].astype(F32)
    sig = jax.nn.sigmoid(gate)
    hid[rows16(f), :] = (gate * sig * up).astype(BF16)
    fa[...] = up * sig * (1.0 + gate * (1.0 - sig))
    fb[...] = gate * sig

    @pl.when(own_diag)
    def _():
        pl.semaphore_wait(bar, 4 + len(plane) + 1)

    @pl.when(jnp.logical_not(own_diag))
    def _():
        pl.semaphore_wait(bar, 4 + len(plane) + 2)

    pending = []

    def perm(h):
        return remote(g_ref.at[:, pl.ds(512 * h, 512)], spread.at[rows16(f)], px_s.at[h], px_r.at[xh], (2 * t + h, z))

    for h in range(2):
        mine = own_diag & (xh == h)

        @pl.when(mine)
        def _():
            pltpu.make_async_copy(g_ref.at[:, pl.ds(512 * h, 512)], spread.at[rows16(f)], loc.at[1]).start()

        @pl.when(jnp.logical_not(mine))
        def _():
            perm(h).start()

    def ag_copy(way, s, b):
        origin = wrap(z - (s - 1)) if way == 0 else wrap(z + (s - 1))
        rows = rows16(2 * origin + (xh if b == 0 else 1 - xh))
        k = (way * 2 + b) * FWD + s - 1
        return remote(hid.at[rows], hid.at[rows], ag_s.at[k], ag_r.at[k], up_z if way == 0 else down_z)

    def ag_recv(way, s, b):
        origin = wrap(z - s) if way == 0 else wrap(z + s)
        rows = rows16(2 * origin + (xh if b == 0 else 1 - xh))
        k = (way * 2 + b) * FWD + s - 1
        remote(hid.at[rows], hid.at[rows], ag_s.at[k], ag_r.at[k], up_z if way == 0 else down_z).wait_recv()

    def hops(way):
        return FWD if way == 0 else BWD

    def ag_step(s):
        for b in range(2):
            for way in range(2):
                if s > 1 and s - 1 <= hops(way):
                    ag_recv(way, s - 1, b)
                if s <= hops(way):
                    c = ag_copy(way, s, b)
                    c.start()
                    pending.append(c)
            if s == 1 and b == 0:
                c = remote(hid.at[rows16(f)], hid.at[rows16(f)], hx_s, hx_r, x_peer)
                c.start()
                pending.append(c)
                other = rows16(2 * z + 1 - xh)
                remote(hid.at[other], hid.at[other], hx_s, hx_r, x_peer).wait_recv()

    ag_step(1)

    for j in range(2):
        mine = own_diag & (xh == j)
        rows = rows16(2 * t + j)

        @pl.when(mine)
        def _():
            pltpu.make_async_copy(g_ref.at[:, pl.ds(512 * j, 512)], spread.at[rows], loc.at[1]).wait()

        @pl.when(jnp.logical_not(mine))
        def _():
            remote(g_ref.at[:, pl.ds(512 * j, 512)], spread.at[rows], px_s.at[j], px_r.at[j], (2 * t + j, z)).wait_recv()

    for r, (dx, dy) in enumerate(plane):
        c = remote(spread.at[rows32(t)], spread.at[rows32(t)], pl_s.at[r], pl_r.at[r], (f, chip(dx, dy) + core))
        c.start()
        pending.append(c)
    c = remote(spread.at[rows32(t)], spread.at[rows32(t)], co_s.at[7], co_r.at[7], core_peer)
    c.start()
    pending.append(c)

    ag_step(2)

    for r, (dx, dy) in enumerate(plane):
        src = rows32(chip(NX - dx, NY - dy) + core)
        remote(spread.at[src], spread.at[src], pl_s.at[r], pl_r.at[r], core_peer).wait_recv()
        c = remote(spread.at[src], spread.at[src], co_s.at[r], co_r.at[r], core_peer)
        c.start()
        pending.append(c)
    ag_step(3)
    for r, (dx, dy) in enumerate(plane + [(0, 0)]):
        src = rows32(chip(NX - dx, NY - dy) + 1 - core)
        remote(spread.at[src], spread.at[src], co_s.at[r], co_r.at[r], core_peer).wait_recv()
    w_copy.wait()

    def matmul(c):
        start, width = COLS[c]
        for i in range(0, width, 256):
            n = min(256, width - i)
            part[c][:, i : i + n] = lax.dot_general(
                spread[...], w_ref[start + i : start + i + n, :], (((1,), (1,)), ((), ())), preferred_element_type=F32
            )

    def rs_target(way, s):
        return wrap(z + FWD + 1 - s) if way == 0 else wrap(z - (BWD + 1 - s))

    def rs_step(s, c):
        for way in range(2):
            if s > hops(way):
                continue
            out = (sf, sb)[way][c].at[s - 1]
            inn = (rf, rb)[way][c]
            total = part[c][rows32(rs_target(way, s)), :]
            if s > 1:
                rs_recv(way, s - 1, c)
                total = total + inn[s - 2].astype(F32)
            out[...] = total.astype(BF16)
            k = (way * 2 + c) * FWD + s - 1
            cp = remote(out, inn.at[s - 1], rs_s.at[k], rs_r.at[k], up_z if way == 0 else down_z)
            cp.start()
            pending.append(cp)

    def rs_recv(way, s, c):
        inn = (rf, rb)[way][c]
        k = (way * 2 + c) * FWD + s - 1
        remote(inn.at[s - 1], inn.at[s - 1], rs_s.at[k], rs_r.at[k], up_z if way == 0 else down_z).wait_recv()

    def gw_tile(i, n):
        gw_ref[i : i + n, :] = lax.dot_general(
            hid[:, i : i + n], spread[...], (((0,), (0,)), ((), ())), preferred_element_type=F32
        ).astype(BF16)
        cp = pltpu.make_async_copy(gw_ref.at[pl.ds(i, n)], gw_hbm.at[pl.ds(i, n)], loc.at[2 + i // 256])
        cp.start()
        out_copies.append(cp)

    out_copies = []
    for c in range(2):
        matmul(c)
        rs_step(1, c)
    ag_step(4)
    tiles = [(i, min(256, 1664 - i)) for i in range(0, 1664, 256)]
    for s in range(2, FWD + 1):
        for c in range(2):
            rs_step(s, c)
        if s + 3 <= FWD + 1:
            ag_step(s + 3)
        else:
            for _ in range(3):
                if tiles:
                    gw_tile(*tiles.pop(0))

    for tile in tiles:
        gw_tile(*tile)

    keep = []
    for c in range(2):
        rs_recv(0, FWD, c)
        rs_recv(1, BWD, c)

        def total(i):
            rows = pl.ds(pl.multiple_of(16 * i, 16), 16)
            return part[c][rows16(2 * z + i), :] + rf[c][FWD - 1, rows, :].astype(F32) + rb[c][BWD - 1, rows, :].astype(F32)

        xsend[c][...] = total(1 - xh).astype(BF16)
        cp = remote(xsend[c], xrecv[c], fx_s.at[c], fx_r.at[c], x_peer)
        cp.start()
        pending.append(cp)
        keep.append(total(xh))
    for c in range(2):
        start, width = COLS[c]
        remote(xsend[c], xrecv[c], fx_s.at[c], fx_r.at[c], x_peer).wait_recv()
        grad = keep[c] + xrecv[c][...].astype(F32)
        gg_ref[:, start : start + width] = (grad * fa[:, start : start + width]).astype(BF16)
        gu_ref[:, start : start + width] = (grad * fb[:, start : start + width]).astype(BF16)

    for cp in out_copies:
        cp.wait()
    for cp in pending:
        cp.wait_send()
    for h in range(2):
        @pl.when(jnp.logical_not(own_diag & (xh == h)))
        def _():
            perm(h).wait_send()


def shards(grad_out, gate_pre, up_pre, down_weight):
    tokens, hidden, model = NZ * 2 * gate_pre.shape[0], gate_pre.shape[1], down_weight.shape[1]
    dma = pltpu.SemaphoreType.DMA
    widths = [w for _, w in COLS]
    return pl.pallas_call(
        kernel,
        out_shape=(
            jax.ShapeDtypeStruct(gate_pre.shape, BF16),
            jax.ShapeDtypeStruct(up_pre.shape, BF16),
            jax.ShapeDtypeStruct(down_weight.shape, BF16),
        ),
        in_specs=[pl.BlockSpec(memory_space=pltpu.VMEM)] * 3 + [pl.BlockSpec(memory_space=pl.ANY)],
        out_specs=(
            pl.BlockSpec(memory_space=pltpu.VMEM),
            pl.BlockSpec(memory_space=pltpu.VMEM),
            pl.BlockSpec(memory_space=pl.ANY),
        ),
        scratch_shapes=[
            pltpu.VMEM((hidden, model), BF16),
            pltpu.VMEM((tokens, hidden), BF16),
            pltpu.VMEM((tokens, model), BF16),
            pltpu.VMEM((tokens, widths[0]), F32),
            pltpu.VMEM((tokens, widths[1]), F32),
            pltpu.VMEM(gate_pre.shape, F32),
            pltpu.VMEM(gate_pre.shape, F32),
            pltpu.VMEM((hidden, model), BF16),
        ]
        + [pltpu.VMEM((n, 32, w), BF16) for n in (FWD, BWD, FWD, BWD) for w in widths]
        + [pltpu.VMEM((16, w), BF16) for _ in range(2) for w in widths]
        + [
            dma((4 * FWD,)), dma((4 * FWD,)), dma((4 * FWD,)), dma((4 * FWD,)),
            dma, dma, dma((2,)), dma((2,)), dma((7,)), dma((7,)), dma((8,)), dma((8,)), dma((2,)), dma((2,)), dma((9,)),
        ],
        compiler_params=pltpu.CompilerParams(collective_id=0, has_side_effects=True, vmem_limit_bytes=40 * 2**20),
        cost_estimate=pl.CostEstimate(flops=4 * tokens * hidden * model, bytes_accessed=2**22, transcendentals=0),
    )(grad_out, gate_pre, up_pre, down_weight)


def solution(mesh):
    placed = (P("fsdp", "tensor"), P("fsdp", "tensor"), P("fsdp", "tensor"), P("tensor", "fsdp"))
    return jax.shard_map(
        shards,
        mesh=mesh,
        in_specs=placed,
        out_specs=(P("fsdp", "tensor"), P("fsdp", "tensor"), P("tensor", "fsdp")),
        check_vma=False,
    )
```

```python
import functools

import jax
import jax.numpy as jnp
from jax import lax
from jax.experimental import pallas as pl
from jax.experimental.pallas import tpu as pltpu
from jax.sharding import PartitionSpec as P

MESH = pl.DeviceIdType.MESH
F32, BF16 = jnp.float32, jnp.bfloat16
NZ, NX, NY = 16, 2, 4
FWD, BWD = 8, 7
CHUNKS = ((0, 384, False), (384, 384, False), (768, 896, True))
TREE = (
    ((0, 8, 7), (0, 3, 2), (1, 7, 6), (1, 2, 1)),
    ((0, 7, 6), (0, 2, 1), (1, 6, 5), (1, 1, 0)),
    ((0, 6, 5), (0, 1, 0), (1, 5, 4)),
    ((0, 5, 4), (1, 4, 3)),
    ((0, 4, 0), (1, 3, 0)),
)
SLOTS = [(way, o) for stage in TREE for way, o, _ in stage]
CROSS = SLOTS + [(0, 0)]
CUTS = (0, len(TREE[0]), len(TREE[0]) + len(TREE[1]), len(CROSS))


def wrap(z):
    return lax.rem(z + 2 * NZ, NZ)


def kernel(
    g_hbm, gate_hbm, up_hbm, w_hbm, gg_ref, gu_ref, gw_hbm,
    g_ref, gate_ref, up_ref, w_ref, hid, spread, fa, fb, gw_ref,
    part0, part1, part2, ts0, ts1, ts2, tr0, tr1, tr2, fs0, fs1, fr0, fr1, xsend, xrecv,
    ag_s, ag_r, t_s, t_r, fx_s, fx_r, x_s, x_r, hx_s, hx_r, px_s, px_r, pl_s, pl_r, co_s, co_r, loc,
):
    f, t = lax.axis_index("fsdp"), lax.axis_index("tensor")
    z, xh = f // 2, lax.rem(f, 2)
    xl, y, core = t // (2 * NY), lax.rem(t // 2, NY), lax.rem(t, 2)
    part, tsend, trecv = (part0, part1, part2), (ts0, ts1, ts2), (tr0, tr1, tr2)
    fsend, frecv = (fs0, fs1), (fr0, fr1)

    loads = [
        pltpu.make_async_copy(src, dst, loc.at[i])
        for i, (src, dst) in enumerate(((gate_hbm, gate_ref), (up_hbm, up_ref), (g_hbm, g_ref), (w_hbm, w_ref)))
    ]
    for cp in loads:
        cp.start()

    def along(d):
        return (2 * wrap(z + d) + xh, t)

    up_z = (2 * wrap(z + 1) + xh, t)
    down_z = (2 * wrap(z - 1) + xh, t)
    x_peer = (2 * z + 1 - xh, t)
    core_peer = (f, t + 1 - 2 * core)
    plane = [(dx, dy) for dx in range(NX) for dy in range(NY) if (dx, dy) != (0, 0)]

    def chip(dx, dy):
        return lax.rem(xl + dx, NX) * 2 * NY + lax.rem(y + dy, NY) * 2

    def rows16(i):
        return pl.ds(pl.multiple_of(16 * i, 16), 16)

    def rows32(i):
        return pl.ds(pl.multiple_of(32 * i, 32), 32)

    def remote(src, dst, ss, rs, dev):
        return pltpu.make_async_remote_copy(
            src_ref=src, dst_ref=dst, send_sem=ss, recv_sem=rs, device_id=dev, device_id_type=MESH
        )

    own_diag = t == z

    bar = pltpu.get_barrier_semaphore()
    reach = sorted({o - p if way == 0 else p - o for stage in TREE for way, o, p in stage} | {1, -1})
    reach = sorted(set(reach) | {-d for d in reach})
    for dev in [along(d) for d in reach] + [x_peer, core_peer] + [(f, chip(dx, dy) + core) for dx, dy in plane]:
        pl.semaphore_signal(bar, inc=1, device_id=dev, device_id_type=MESH)
    for h in range(2):
        @pl.when(jnp.logical_not(own_diag & (xh == h)))
        def _():
            pl.semaphore_signal(bar, inc=1, device_id=(2 * t + h, z), device_id_type=MESH)

    loads[0].wait()
    loads[1].wait()
    gate, up = gate_ref[...].astype(F32), up_ref[...].astype(F32)
    sig = jax.nn.sigmoid(gate)
    hid[rows16(f), :] = (gate * sig * up).astype(BF16)
    fa[...] = up * sig * (1.0 + gate * (1.0 - sig))
    fb[...] = gate * sig

    @pl.when(own_diag)
    def _():
        pl.semaphore_wait(bar, len(reach) + 2 + len(plane) + 1)

    @pl.when(jnp.logical_not(own_diag))
    def _():
        pl.semaphore_wait(bar, len(reach) + 2 + len(plane) + 2)

    pending = []
    loads[2].wait()

    def perm(h):
        return remote(g_ref.at[:, pl.ds(512 * h, 512)], spread.at[rows16(f)], px_s.at[h], px_r.at[xh], (2 * t + h, z))

    for h in range(2):
        mine = own_diag & (xh == h)

        @pl.when(mine)
        def _():
            pltpu.make_async_copy(g_ref.at[:, pl.ds(512 * h, 512)], spread.at[rows16(f)], loc.at[4]).start()

        @pl.when(jnp.logical_not(mine))
        def _():
            perm(h).start()

    def ag_copy(way, s):
        rows = rows16(2 * (wrap(z - (s - 1)) if way == 0 else wrap(z + (s - 1))) + xh)
        k = way * FWD + s - 1
        return remote(hid.at[rows], hid.at[rows], ag_s.at[k], ag_r.at[k], up_z if way == 0 else down_z)

    def ag_arrived(way, s):
        rows = rows16(2 * (wrap(z - s) if way == 0 else wrap(z + s)) + xh)
        k = way * FWD + s - 1
        remote(hid.at[rows], hid.at[rows], ag_s.at[k], ag_r.at[k], up_z if way == 0 else down_z).wait_recv()

    def hid_x(way, s, h):
        rows = rows16(2 * (wrap(z - s) if way == 0 else wrap(z + s)) + h)
        k = way * FWD + s
        return remote(hid.at[rows], hid.at[rows], hx_s.at[k], hx_r.at[k], x_peer)

    def hops(way):
        return FWD if way == 0 else BWD

    def ag_step(s):
        for way in range(2):
            came = s - 1 <= hops(way) and (s > 1 or way == 0)
            if s > 1 and came:
                ag_arrived(way, s - 1)
            if s <= hops(way):
                c = ag_copy(way, s)
                c.start()
                pending.append(c)
            if came:
                c = hid_x(way, s - 1, xh)
                c.start()
                pending.append(c)

    ag_step(1)
    ag_step(2)

    for j in range(2):
        mine = own_diag & (xh == j)
        rows = rows16(2 * t + j)

        @pl.when(mine)
        def _():
            pltpu.make_async_copy(g_ref.at[:, pl.ds(512 * j, 512)], spread.at[rows], loc.at[4]).wait()

        @pl.when(jnp.logical_not(mine))
        def _():
            remote(g_ref.at[:, pl.ds(512 * j, 512)], spread.at[rows], px_s.at[j], px_r.at[j], (2 * t + j, z)).wait_recv()

    for r, (dx, dy) in enumerate(plane):
        c = remote(spread.at[rows32(t)], spread.at[rows32(t)], pl_s.at[r], pl_r.at[r], (f, chip(dx, dy) + core))
        c.start()
        pending.append(c)
    c = remote(spread.at[rows32(t)], spread.at[rows32(t)], co_s.at[7], co_r.at[7], core_peer)
    c.start()
    pending.append(c)

    ag_step(3)

    for r, (dx, dy) in enumerate(plane):
        src = rows32(chip(NX - dx, NY - dy) + core)
        remote(spread.at[src], spread.at[src], pl_s.at[r], pl_r.at[r], core_peer).wait_recv()
        c = remote(spread.at[src], spread.at[src], co_s.at[r], co_r.at[r], core_peer)
        c.start()
        pending.append(c)
    ag_step(4)
    for r, (dx, dy) in enumerate(plane + [(0, 0)]):
        src = rows32(chip(NX - dx, NY - dy) + 1 - core)
        remote(spread.at[src], spread.at[src], co_s.at[r], co_r.at[r], core_peer).wait_recv()
    loads[3].wait()

    def matmul(c):
        start, width, _ = CHUNKS[c]
        for i in range(0, width, 256):
            n = min(256, width - i)
            part[c][:, i : i + n] = lax.dot_general(
                spread[...], w_ref[start + i : start + i + n, :], (((1,), (1,)), ((), ())), preferred_element_type=F32
            )

    def dest(way, o):
        return wrap(z + o) if way == 0 else wrap(z - o)

    def hop(c, way, o, p):
        i, d = SLOTS.index((way, o)), o - p if way == 0 else p - o
        return remote(tsend[c].at[i], trecv[c].at[i], t_s.at[c, i], t_r.at[c, i], along(d))

    def cross(g):
        at = pl.ds(CUTS[g], CUTS[g + 1] - CUTS[g])
        return remote(xsend.at[at], xrecv.at[at], x_s.at[g], x_r.at[g], x_peer)

    def cross_x(c):
        for g in range(3):
            for i in range(CUTS[g], CUTS[g + 1]):
                xsend[i] = part[c][rows16(2 * dest(*CROSS[i]) + 1 - xh), :].astype(BF16)
            cross(g).start()
            pending.append(cross(g))

    def gathered(c, way, o):
        if CHUNKS[c][2]:
            total = part[c][rows16(2 * dest(way, o) + xh), :] + xrecv[CROSS.index((way, o))].astype(F32)
        else:
            total = part[c][rows32(dest(way, o)), :]
        for stage in TREE:
            for w, k, p in stage:
                if p == o and (w == way or o == 0):
                    hop(c, w, k, p).wait_recv()
                    total = total + trecv[c][SLOTS.index((w, k))].astype(F32)
        return total

    def tree_stage(n, c):
        if CHUNKS[c][2] and n < 3:
            cross(n).wait_recv()
        for way, o, p in TREE[n]:
            tsend[c][SLOTS.index((way, o))] = gathered(c, way, o).astype(BF16)
            cp = hop(c, way, o, p)
            cp.start()
            pending.append(cp)

    def gw_tile(i, n):
        gw_ref[i : i + n, :] = lax.dot_general(
            hid[:, i : i + n], spread[...], (((0,), (0,)), ((), ())), preferred_element_type=F32
        ).astype(BF16)
        cp = pltpu.make_async_copy(gw_ref.at[pl.ds(i, n)], gw_hbm.at[pl.ds(i, n)], loc.at[5 + i // 256])
        cp.start()
        out_copies.append(cp)

    out_copies = []
    matmul(2)
    cross_x(2)
    for c in range(2):
        matmul(c)
        tree_stage(0, c)
    ag_step(5)
    for n in range(1, len(TREE)):
        for c in range(2):
            tree_stage(n, c)
        tree_stage(n - 1, 2)
        if n + 5 <= FWD + 1:
            ag_step(n + 5)
    tree_stage(len(TREE) - 1, 2)
    for n in range(len(TREE) + 5, FWD + 2):
        ag_step(n)
    for way in range(2):
        for n in range(0 if way == 0 else 1, hops(way) + 1):
            hid_x(way, n, 1 - xh).wait_recv()
    for i in range(0, 1664, 256):
        gw_tile(i, min(256, 1664 - i))

    def final(c):
        return remote(fsend[c].at[1 - xh], frecv[c], fx_s.at[c], fx_r.at[c], x_peer)

    def gradients(c, grad):
        cols = pl.ds(CHUNKS[c][0], CHUNKS[c][1])
        gg_ref[:, cols] = (grad * fa[:, cols]).astype(BF16)
        gu_ref[:, cols] = (grad * fb[:, cols]).astype(BF16)

    for c in range(2):
        total = gathered(c, 0, 0)
        fsend[c][0], fsend[c][1] = total[:16], total[16:]
        final(c).start()
        pending.append(final(c))
    for c in range(2):
        final(c).wait_recv()
        grad = fsend[c][xh] + frecv[c][...]
        gradients(c, grad)
    gradients(2, gathered(2, 0, 0))

    for cp in out_copies:
        cp.wait()
    for cp in pending:
        cp.wait_send()
    for h in range(2):
        @pl.when(jnp.logical_not(own_diag & (xh == h)))
        def _():
            perm(h).wait_send()


def shards(grad_out, gate_pre, up_pre, down_weight):
    tokens, hidden, model = NZ * 2 * gate_pre.shape[0], gate_pre.shape[1], down_weight.shape[1]
    dma = pltpu.SemaphoreType.DMA
    widths = [w for _, w, _ in CHUNKS]
    heights = [16 if x_first else 32 for _, _, x_first in CHUNKS]
    return pl.pallas_call(
        kernel,
        out_shape=(
            jax.ShapeDtypeStruct(gate_pre.shape, BF16),
            jax.ShapeDtypeStruct(up_pre.shape, BF16),
            jax.ShapeDtypeStruct(down_weight.shape, BF16),
        ),
        in_specs=[pl.BlockSpec(memory_space=pltpu.HBM)] * 4,
        out_specs=(
            pl.BlockSpec(memory_space=pltpu.VMEM),
            pl.BlockSpec(memory_space=pltpu.VMEM),
            pl.BlockSpec(memory_space=pl.ANY),
        ),
        scratch_shapes=[
            pltpu.VMEM(grad_out.shape, BF16),
            pltpu.VMEM(gate_pre.shape, BF16),
            pltpu.VMEM(up_pre.shape, BF16),
            pltpu.VMEM((hidden, model), BF16),
            pltpu.VMEM((tokens, hidden), BF16),
            pltpu.VMEM((tokens, model), BF16),
            pltpu.VMEM(gate_pre.shape, F32),
            pltpu.VMEM(gate_pre.shape, F32),
            pltpu.VMEM((hidden, model), BF16),
        ]
        + [pltpu.VMEM((tokens, w), F32) for w in widths]
        + [pltpu.VMEM((15, h, w), BF16) for _ in range(2) for h, w in zip(heights, widths)]
        + [pltpu.VMEM((2, 16, w), F32) for w in widths[:2]]
        + [pltpu.VMEM((16, w), F32) for w in widths[:2]]
        + [pltpu.VMEM((16, 16, widths[2]), BF16)] * 2
        + [
            dma((2 * FWD,)), dma((2 * FWD,)), dma((3, 15)), dma((3, 15)), dma((2,)), dma((2,)), dma((3,)), dma((3,)),
            dma((2 * FWD,)), dma((2 * FWD,)), dma((2,)), dma((2,)), dma((7,)), dma((7,)), dma((8,)), dma((8,)), dma((12,)),
        ],
        compiler_params=pltpu.CompilerParams(collective_id=0, has_side_effects=True, vmem_limit_bytes=40 * 2**20),
        cost_estimate=pl.CostEstimate(flops=4 * tokens * hidden * model, bytes_accessed=2**22, transcendentals=0),
    )(grad_out, gate_pre, up_pre, down_weight)


def solution(mesh):
    placed = (P("fsdp", "tensor"), P("fsdp", "tensor"), P("fsdp", "tensor"), P("tensor", "fsdp"))
    return jax.shard_map(
        shards,
        mesh=mesh,
        in_specs=placed,
        out_specs=(P("fsdp", "tensor"), P("fsdp", "tensor"), P("tensor", "fsdp")),
        check_vma=False,
    )
```

```python
import functools

import jax
import jax.numpy as jnp
from jax import lax
from jax.experimental import pallas as pl
from jax.experimental.pallas import tpu as pltpu
from jax.sharding import PartitionSpec as P

MESH = pl.DeviceIdType.MESH
F32, BF16 = jnp.float32, jnp.bfloat16
NZ, NX, NY = 16, 2, 4
FWD, BWD = 8, 7
CHUNKS = ((0, 384, False), (384, 384, False), (768, 896, True))
TREE = (((0, 8, 7), (0, 2, 1), (1, 7, 6), (1, 1, 0)), ((0, 7, 6), (0, 1, 0), (1, 6, 5)), ((0, 6, 5), (1, 5, 4)), ((0, 5, 4), (1, 4, 3)), ((0, 4, 3), (1, 3, 2)), ((0, 3, 0), (1, 2, 0)))
SLOTS = [(way, o) for stage in TREE for way, o, _ in stage]
CROSS = SLOTS + [(0, 0)]
CUTS = (0, len(TREE[0]), len(TREE[0]) + len(TREE[1]), len(CROSS))


def wrap(z):
    return lax.rem(z + 2 * NZ, NZ)


def kernel(
    g_hbm, gate_hbm, up_hbm, w_hbm, gg_ref, gu_ref, gw_hbm,
    g_ref, gate_ref, up_ref, w_ref, hid, spread, fa, fb, gw_ref,
    part0, part1, part2, ts0, ts1, ts2, tr0, tr1, tr2, fs0, fs1, fr0, fr1, xsend, xrecv,
    ag_s, ag_r, t_s, t_r, fx_s, fx_r, x_s, x_r, hx_s, hx_r, px_s, px_r, pl_s, pl_r, co_s, co_r, loc,
):
    f, t = lax.axis_index("fsdp"), lax.axis_index("tensor")
    z, xh = f // 2, lax.rem(f, 2)
    xl, y, core = t // (2 * NY), lax.rem(t // 2, NY), lax.rem(t, 2)
    part, tsend, trecv = (part0, part1, part2), (ts0, ts1, ts2), (tr0, tr1, tr2)
    fsend, frecv = (fs0, fs1), (fr0, fr1)

    loads = [
        pltpu.make_async_copy(src, dst, loc.at[i])
        for i, (src, dst) in enumerate(((gate_hbm, gate_ref), (up_hbm, up_ref), (g_hbm, g_ref), (w_hbm, w_ref)))
    ]
    for cp in loads:
        cp.start()

    def along(d):
        return (2 * wrap(z + d) + xh, t)

    up_z = (2 * wrap(z + 1) + xh, t)
    down_z = (2 * wrap(z - 1) + xh, t)
    x_peer = (2 * z + 1 - xh, t)
    core_peer = (f, t + 1 - 2 * core)
    plane = [(dx, dy) for dx in range(NX) for dy in range(NY) if (dx, dy) != (0, 0)]

    def chip(dx, dy):
        return lax.rem(xl + dx, NX) * 2 * NY + lax.rem(y + dy, NY) * 2

    def rows16(i):
        return pl.ds(pl.multiple_of(16 * i, 16), 16)

    def rows32(i):
        return pl.ds(pl.multiple_of(32 * i, 32), 32)

    def remote(src, dst, ss, rs, dev):
        return pltpu.make_async_remote_copy(
            src_ref=src, dst_ref=dst, send_sem=ss, recv_sem=rs, device_id=dev, device_id_type=MESH
        )

    own_diag = t == z

    bar = pltpu.get_barrier_semaphore()
    reach = sorted({o - p if way == 0 else p - o for stage in TREE for way, o, p in stage} | {1, -1})
    reach = sorted(set(reach) | {-d for d in reach})
    for dev in [along(d) for d in reach] + [x_peer, core_peer] + [(f, chip(dx, dy) + core) for dx, dy in plane]:
        pl.semaphore_signal(bar, inc=1, device_id=dev, device_id_type=MESH)
    for h in range(2):
        @pl.when(jnp.logical_not(own_diag & (xh == h)))
        def _():
            pl.semaphore_signal(bar, inc=1, device_id=(2 * t + h, z), device_id_type=MESH)

    loads[0].wait()
    loads[1].wait()
    gate, up = gate_ref[...].astype(F32), up_ref[...].astype(F32)
    sig = jax.nn.sigmoid(gate)
    hid[rows16(f), :] = (gate * sig * up).astype(BF16)
    fa[...] = up * sig * (1.0 + gate * (1.0 - sig))
    fb[...] = gate * sig

    @pl.when(own_diag)
    def _():
        pl.semaphore_wait(bar, len(reach) + 2 + len(plane) + 1)

    @pl.when(jnp.logical_not(own_diag))
    def _():
        pl.semaphore_wait(bar, len(reach) + 2 + len(plane) + 2)

    pending = []
    loads[2].wait()

    def perm(h):
        return remote(g_ref.at[:, pl.ds(512 * h, 512)], spread.at[rows16(f)], px_s.at[h], px_r.at[xh], (2 * t + h, z))

    for h in range(2):
        mine = own_diag & (xh == h)

        @pl.when(mine)
        def _():
            pltpu.make_async_copy(g_ref.at[:, pl.ds(512 * h, 512)], spread.at[rows16(f)], loc.at[4]).start()

        @pl.when(jnp.logical_not(mine))
        def _():
            perm(h).start()

    def ag_copy(way, s):
        rows = rows16(2 * (wrap(z - (s - 1)) if way == 0 else wrap(z + (s - 1))) + xh)
        k = way * FWD + s - 1
        return remote(hid.at[rows], hid.at[rows], ag_s.at[k], ag_r.at[k], up_z if way == 0 else down_z)

    def ag_arrived(way, s):
        rows = rows16(2 * (wrap(z - s) if way == 0 else wrap(z + s)) + xh)
        k = way * FWD + s - 1
        remote(hid.at[rows], hid.at[rows], ag_s.at[k], ag_r.at[k], up_z if way == 0 else down_z).wait_recv()

    def hid_x(way, s, h):
        rows = rows16(2 * (wrap(z - s) if way == 0 else wrap(z + s)) + h)
        k = way * FWD + s
        return remote(hid.at[rows], hid.at[rows], hx_s.at[k], hx_r.at[k], x_peer)

    def hops(way):
        return FWD if way == 0 else BWD

    def ag_step(s):
        for way in range(2):
            came = s - 1 <= hops(way) and (s > 1 or way == 0)
            if s > 1 and came:
                ag_arrived(way, s - 1)
            if s <= hops(way):
                c = ag_copy(way, s)
                c.start()
                pending.append(c)
            if came:
                c = hid_x(way, s - 1, xh)
                c.start()
                pending.append(c)

    ag_step(1)
    ag_step(2)

    for j in range(2):
        mine = own_diag & (xh == j)
        rows = rows16(2 * t + j)

        @pl.when(mine)
        def _():
            pltpu.make_async_copy(g_ref.at[:, pl.ds(512 * j, 512)], spread.at[rows], loc.at[4]).wait()

        @pl.when(jnp.logical_not(mine))
        def _():
            remote(g_ref.at[:, pl.ds(512 * j, 512)], spread.at[rows], px_s.at[j], px_r.at[j], (2 * t + j, z)).wait_recv()

    for r, (dx, dy) in enumerate(plane):
        c = remote(spread.at[rows32(t)], spread.at[rows32(t)], pl_s.at[r], pl_r.at[r], (f, chip(dx, dy) + core))
        c.start()
        pending.append(c)
    c = remote(spread.at[rows32(t)], spread.at[rows32(t)], co_s.at[7], co_r.at[7], core_peer)
    c.start()
    pending.append(c)

    ag_step(3)

    for r, (dx, dy) in enumerate(plane):
        src = rows32(chip(NX - dx, NY - dy) + core)
        remote(spread.at[src], spread.at[src], pl_s.at[r], pl_r.at[r], core_peer).wait_recv()
        c = remote(spread.at[src], spread.at[src], co_s.at[r], co_r.at[r], core_peer)
        c.start()
        pending.append(c)
    ag_step(4)
    for r, (dx, dy) in enumerate(plane + [(0, 0)]):
        src = rows32(chip(NX - dx, NY - dy) + 1 - core)
        remote(spread.at[src], spread.at[src], co_s.at[r], co_r.at[r], core_peer).wait_recv()
    loads[3].wait()

    def matmul(c):
        start, width, _ = CHUNKS[c]
        for i in range(0, width, 256):
            n = min(256, width - i)
            part[c][:, i : i + n] = lax.dot_general(
                spread[...], w_ref[start + i : start + i + n, :], (((1,), (1,)), ((), ())), preferred_element_type=F32
            )

    def dest(way, o):
        return wrap(z + o) if way == 0 else wrap(z - o)

    def hop(c, way, o, p):
        i, d = SLOTS.index((way, o)), o - p if way == 0 else p - o
        return remote(tsend[c].at[i], trecv[c].at[i], t_s.at[c, i], t_r.at[c, i], along(d))

    def cross(g):
        at = pl.ds(CUTS[g], CUTS[g + 1] - CUTS[g])
        return remote(xsend.at[at], xrecv.at[at], x_s.at[g], x_r.at[g], x_peer)

    def cross_x(c):
        for g in range(3):
            for i in range(CUTS[g], CUTS[g + 1]):
                xsend[i] = part[c][rows16(2 * dest(*CROSS[i]) + 1 - xh), :].astype(BF16)
            cross(g).start()
            pending.append(cross(g))

    def gathered(c, way, o):
        if CHUNKS[c][2]:
            total = part[c][rows16(2 * dest(way, o) + xh), :] + xrecv[CROSS.index((way, o))].astype(F32)
        else:
            total = part[c][rows32(dest(way, o)), :]
        for stage in TREE:
            for w, k, p in stage:
                if p == o and (w == way or o == 0):
                    hop(c, w, k, p).wait_recv()
                    total = total + trecv[c][SLOTS.index((w, k))].astype(F32)
        return total

    def tree_stage(n, c):
        if CHUNKS[c][2] and n < 3:
            cross(n).wait_recv()
        for way, o, p in TREE[n]:
            tsend[c][SLOTS.index((way, o))] = gathered(c, way, o).astype(BF16)
            cp = hop(c, way, o, p)
            cp.start()
            pending.append(cp)

    def gw_tile(i, n):
        gw_ref[i : i + n, :] = lax.dot_general(
            hid[:, i : i + n], spread[...], (((0,), (0,)), ((), ())), preferred_element_type=F32
        ).astype(BF16)
        cp = pltpu.make_async_copy(gw_ref.at[pl.ds(i, n)], gw_hbm.at[pl.ds(i, n)], loc.at[5 + i // 256])
        cp.start()
        out_copies.append(cp)

    out_copies = []
    matmul(2)
    cross_x(2)
    for c in range(2):
        matmul(c)
        tree_stage(0, c)
    ag_step(5)
    for n in range(1, len(TREE)):
        for c in range(2):
            tree_stage(n, c)
        tree_stage(n - 1, 2)
        if n + 5 <= FWD + 1:
            ag_step(n + 5)
    tree_stage(len(TREE) - 1, 2)
    for n in range(len(TREE) + 5, FWD + 2):
        ag_step(n)
    for way in range(2):
        for n in range(0 if way == 0 else 1, hops(way) + 1):
            hid_x(way, n, 1 - xh).wait_recv()
    for i in range(0, 1664, 256):
        gw_tile(i, min(256, 1664 - i))

    def final(c):
        return remote(fsend[c].at[1 - xh], frecv[c], fx_s.at[c], fx_r.at[c], x_peer)

    def gradients(c, grad):
        cols = pl.ds(CHUNKS[c][0], CHUNKS[c][1])
        gg_ref[:, cols] = (grad * fa[:, cols]).astype(BF16)
        gu_ref[:, cols] = (grad * fb[:, cols]).astype(BF16)

    for c in range(2):
        total = gathered(c, 0, 0)
        fsend[c][0], fsend[c][1] = total[:16], total[16:]
        final(c).start()
        pending.append(final(c))
    for c in range(2):
        final(c).wait_recv()
        grad = fsend[c][xh] + frecv[c][...]
        gradients(c, grad)
    gradients(2, gathered(2, 0, 0))

    for cp in out_copies:
        cp.wait()
    for cp in pending:
        cp.wait_send()
    for h in range(2):
        @pl.when(jnp.logical_not(own_diag & (xh == h)))
        def _():
            perm(h).wait_send()


def shards(grad_out, gate_pre, up_pre, down_weight):
    tokens, hidden, model = NZ * 2 * gate_pre.shape[0], gate_pre.shape[1], down_weight.shape[1]
    dma = pltpu.SemaphoreType.DMA
    widths = [w for _, w, _ in CHUNKS]
    heights = [16 if x_first else 32 for _, _, x_first in CHUNKS]
    return pl.pallas_call(
        kernel,
        out_shape=(
            jax.ShapeDtypeStruct(gate_pre.shape, BF16),
            jax.ShapeDtypeStruct(up_pre.shape, BF16),
            jax.ShapeDtypeStruct(down_weight.shape, BF16),
        ),
        in_specs=[pl.BlockSpec(memory_space=pltpu.HBM)] * 4,
        out_specs=(
            pl.BlockSpec(memory_space=pltpu.VMEM),
            pl.BlockSpec(memory_space=pltpu.VMEM),
            pl.BlockSpec(memory_space=pl.ANY),
        ),
        scratch_shapes=[
            pltpu.VMEM(grad_out.shape, BF16),
            pltpu.VMEM(gate_pre.shape, BF16),
            pltpu.VMEM(up_pre.shape, BF16),
            pltpu.VMEM((hidden, model), BF16),
            pltpu.VMEM((tokens, hidden), BF16),
            pltpu.VMEM((tokens, model), BF16),
            pltpu.VMEM(gate_pre.shape, F32),
            pltpu.VMEM(gate_pre.shape, F32),
            pltpu.VMEM((hidden, model), BF16),
        ]
        + [pltpu.VMEM((tokens, w), F32) for w in widths]
        + [pltpu.VMEM((15, h, w), BF16) for _ in range(2) for h, w in zip(heights, widths)]
        + [pltpu.VMEM((2, 16, w), F32) for w in widths[:2]]
        + [pltpu.VMEM((16, w), F32) for w in widths[:2]]
        + [pltpu.VMEM((16, 16, widths[2]), BF16)] * 2
        + [
            dma((2 * FWD,)), dma((2 * FWD,)), dma((3, 15)), dma((3, 15)), dma((2,)), dma((2,)), dma((3,)), dma((3,)),
            dma((2 * FWD,)), dma((2 * FWD,)), dma((2,)), dma((2,)), dma((7,)), dma((7,)), dma((8,)), dma((8,)), dma((12,)),
        ],
        compiler_params=pltpu.CompilerParams(collective_id=0, has_side_effects=True, vmem_limit_bytes=52 * 2**20),
        cost_estimate=pl.CostEstimate(flops=4 * tokens * hidden * model, bytes_accessed=2**22, transcendentals=0),
    )(grad_out, gate_pre, up_pre, down_weight)


def solution(mesh):
    placed = (P("fsdp", "tensor"), P("fsdp", "tensor"), P("fsdp", "tensor"), P("tensor", "fsdp"))
    return jax.shard_map(
        shards,
        mesh=mesh,
        in_specs=placed,
        out_specs=(P("fsdp", "tensor"), P("fsdp", "tensor"), P("tensor", "fsdp")),
        check_vma=False,
    )
```
